32 devices in a mesh: row: 4 (over z), col: 8 (over y, x, core).
Axes of the slice: x: 2, y: 2, z: 4, core: 2. Of those that a mesh axis runs over, the one named last changes fastest.
Arguments:
- t_amps: bfloat16 [3, 4096, 4096], P(None, ('row', 'col')), may hold values from -0.099609375 to 0.099609375
- w_cycle: bfloat16 [3, 4096, 4096], P(None, ('row', 'col')), may hold values from -3 to 3
- v_cycle: bfloat16 [3, 4096, 4096], P(None, ('row', 'col')), may hold values from -6 to 6
- occ_irrep: int32 [50], replicated, may hold values from 0 to 7, as said below
- vir_irrep: int32 [500], replicated, may hold values from 0 to 7, as said below
- e_occ: float32 [50], replicated, may hold values from -2.5 to -0.5
- e_vir: float32 [500], replicated, may hold values from 0.5 to 3
Outputs:
- t_new: float32 [3, 4096, 4096], P(None, ('row', 'col'))
The draws below stay inside these ranges and needn't reach their ends.
Inputs may be any that keep to these rules, and one draw needn't show every extreme that they name: `occ_irrep`: a random permutation of a label table in which irrep h holds floor(50 * c_h / 50) - floor(50 * c_(h-1) / 50) orbitals, with cumulative c = 12, 16, 24, 29, 33, 39, 45, 50 for h = 0 to 7. `vir_irrep`: a random permutation of a label table in which irrep h holds floor(500 * c_h / 500) - floor(500 * c_(h-1) / 500) orbitals, with cumulative c = 100, 145, 220, 275, 315, 380, 445, 500 for h = 0 to 7.
All inputs are finite; a program needn't handle non-finite values.
Results may differ from the reference program's by a relative error of at most 0.0035.
Values may be sent and summed in bfloat16 or wider, within the bound.
A program may use at most 192 MiB of HBM per device.

```python
import jax
import jax.numpy as jnp

O = 50
V = 500
CAP = 4096
SYMS = 3


def label_table(key, total, bounds, whole):
    index = jnp.arange(total, dtype=jnp.int32)
    edges = jnp.array(bounds, dtype=jnp.int32) * total // whole
    labels = jnp.sum((index[:, None] >= edges[None, :]).astype(jnp.int32), axis=1)
    return jax.random.permutation(key, labels).astype(jnp.int32)


def draw_occ_irrep(key, part):
    key = jax.random.fold_in(key, 11)
    return label_table(key, O, [12, 16, 24, 29, 33, 39, 45], 50)


def draw_vir_irrep(key, part):
    key = jax.random.fold_in(key, 23)
    return label_table(key, V, [100, 145, 220, 275, 315, 380, 445], 500)


def levels(own_key, shape, pieces, smallest, top_value):
    factor_of, own = 1.0, jax.random.fold_in(own_key, 6)
    for position, blocks in pieces:
        steps = jnp.exp(jax.random.uniform(jax.random.fold_in(own, position), (blocks,), jnp.float32, smallest / len(pieces), top_value / len(pieces)))
        factor_of = factor_of * jnp.repeat(steps, shape[position] // blocks).reshape([-1 if axis == position else 1 for axis in range(len(shape))])
    return factor_of


def gaussian(rng, extent, spread, bound, shards=(), kind=jnp.bfloat16):
    level = levels(rng, extent, shards, -0.22, 0.18) if shards else 1.0
    entries = jax.random.normal(rng, extent, jnp.float32) * spread * level
    return jnp.minimum(jnp.maximum(entries, -bound), bound).astype(kind)


def setup_inputs(seed: int = 0) -> dict:
    key_list = jax.random.split(jax.random.key(seed), 8)
    t_amps = gaussian(key_list[0], (SYMS, CAP, CAP), 0.015625, 0.099609375, ((1, 32),))
    w_cycle = gaussian(key_list[1], (SYMS, CAP, CAP), 0.5, 3.0, ((1, 32),))
    v_cycle = gaussian(key_list[2], (SYMS, CAP, CAP), 1.0, 6.0, ((1, 32),))
    occ_irrep = draw_occ_irrep(jax.random.fold_in(key_list[7], 71), 0)
    vir_irrep = draw_vir_irrep(jax.random.fold_in(key_list[7], 71), 0)
    e_occ = jnp.clip(jax.random.uniform(key_list[5], (O,), jnp.float32, -2.5, -0.5), -2.5, -0.5)
    e_vir = jnp.clip(jax.random.uniform(key_list[6], (V,), jnp.float32, 0.5, 3.0), 0.5, 3.0)
    return dict(t_amps=t_amps, w_cycle=w_cycle, v_cycle=v_cycle, occ_irrep=occ_irrep, vir_irrep=vir_irrep, e_occ=e_occ, e_vir=e_vir)


def pair_table(occ_irrep, vir_irrep, e_occ, e_vir, blocks, slots):
    sym = jnp.bitwise_xor(vir_irrep[:, None], occ_irrep[None, :]).reshape(-1)
    energy = (e_occ[None, :] - e_vir[:, None]).reshape(-1)
    tables = []
    counts = []
    for group in range(blocks):
        hit = (sym == group).astype(jnp.int32)
        rank = jnp.cumsum(hit) - 1
        target = jnp.where(hit > 0, rank, slots).astype(jnp.int32)
        tables.append(jnp.full((slots,), -1.0, jnp.float32).at[target].set(energy, mode="drop"))
        counts.append(jnp.sum(hit))
    return jnp.stack(tables), jnp.stack(counts)


def reference(t_amps, w_cycle, v_cycle, occ_irrep, vir_irrep, e_occ, e_vir):
    pair_energy, counts = pair_table(occ_irrep, vir_irrep, e_occ, e_vir, SYMS, CAP)
    slot = jnp.arange(CAP, dtype=jnp.int32)
    results = []
    for group in range(SYMS):
        alive = slot < counts[group]
        live = alive[:, None] & alive[None, :]
        tm = jnp.where(live, t_amps[group], jnp.zeros((), jnp.bfloat16))
        wm = jnp.where(live, w_cycle[group], jnp.zeros((), jnp.bfloat16))
        vm = jnp.where(live, v_cycle[group], jnp.zeros((), jnp.bfloat16))
        x_cycle = (wm.astype(jnp.float32) + 0.5 * jnp.dot(vm, tm, preferred_element_type=jnp.float32)).astype(jnp.bfloat16)
        z_cycle = jnp.dot(tm, x_cycle, preferred_element_type=jnp.float32)
        numer = vm.astype(jnp.float32) + z_cycle + z_cycle.T
        denom = pair_energy[group][:, None] + pair_energy[group][None, :]
        results.append(jnp.where(live, numer / denom, jnp.zeros((), jnp.float32)))
    return jnp.stack(results)
```

```python
import functools

import jax
import jax.numpy as jnp
from jax import lax
from jax.experimental import pallas as pl
from jax.experimental.pallas import tpu as pltpu
from jax.sharding import PartitionSpec as P

OCC_CUM = (12, 16, 24, 29, 33, 39, 45, 50)
VIR_CUM = (100, 145, 220, 275, 315, 380, 445, 500)
MESH = pl.DeviceIdType.MESH


def block_counts(n_occ, n_vir, blocks):
    occ = [n_occ * c // 50 for c in OCC_CUM]
    vir = [n_vir * c // 500 for c in VIR_CUM]
    occ = [b - a for a, b in zip([0] + occ, occ)]
    vir = [b - a for a, b in zip([0] + vir, vir)]
    return [sum(occ[h] * vir[h ^ g] for h in range(8)) for g in range(blocks)]


def pair_table(occ_irrep, vir_irrep, e_occ, e_vir, counts, slots):
    blocks = len(counts)
    n_occ = occ_irrep.shape[0]
    group = jnp.arange(blocks, dtype=jnp.int32)
    want = jnp.bitwise_xor(vir_irrep[None, :], group[:, None])
    per = jnp.sum((want[:, :, None] == occ_irrep[None, None, :]).astype(jnp.int32), axis=2)
    n_vir = vir_irrep.shape[0]
    before = jnp.arange(n_vir)[:, None] < jnp.arange(n_vir)[None, :]
    first = jnp.sum(jnp.where(before[None], per[:, :, None], 0), axis=1)
    slot = jnp.arange(slots, dtype=jnp.int32)[None, None, :]
    offset = slot - first[:, :, None]
    hit = (offset >= 0) & (offset < per[:, :, None])
    place = jnp.sum(jnp.where(hit, offset * 8 + want[:, :, None], 0), axis=1)
    e_a = jnp.sum(jnp.where(hit, e_vir[None, :, None], 0.0), axis=1)
    earlier = jnp.arange(n_occ)[:, None] < jnp.arange(n_occ)[None, :]
    rank = jnp.sum((earlier & (occ_irrep[:, None] == occ_irrep[None, :])).astype(jnp.int32), axis=0)
    key = rank * 8 + occ_irrep
    e_i = jnp.sum(
        jnp.where(place[:, None, :] == key[None, :, None], e_occ[None, :, None], 0.0), axis=1
    )
    filled = slot[0] < jnp.array(counts, jnp.int32)[:, None]
    return jnp.where(filled, e_i - e_a, -1.0)


class Plan:
    def __init__(self, mesh, shape, counts):
        self.nr, self.nc = mesh.shape["row"], mesh.shape["col"]
        self.blocks, self.slots = shape[0], shape[2]
        self.own = self.slots // (self.nr * self.nc)
        self.panel = self.own * self.nc
        self.counts = counts
        self.depth = [-(-n // 128) * 128 for n in counts]
        self.width = [-(-k // (128 * self.nc)) * 128 for k in self.depth]


def barrier_line(plan, r, c):
    sem = pltpu.get_barrier_semaphore()
    for o in range(1, plan.nc):
        pl.semaphore_signal(
            sem, inc=1, device_id=(r, lax.rem(c + o, plan.nc)), device_id_type=MESH
        )
    for o in range(1, plan.nr):
        pl.semaphore_signal(
            sem, inc=1, device_id=(lax.rem(r + o, plan.nr), c), device_id_type=MESH
        )
    pl.semaphore_wait(sem, plan.nc + plan.nr - 2)


def remote(src, dst, send, recv, device):
    return pltpu.make_async_remote_copy(
        src_ref=src, dst_ref=dst, send_sem=send, recv_sem=recv, device_id=device, device_id_type=MESH
    )


class Spread:
    def __init__(self, plan, g, r, c, src, dst, base, send, recv, local):
        self.plan, self.g, self.r, self.c = plan, g, r, c
        self.src, self.dst, self.base = src, dst, base
        self.send, self.recv, self.local = send, recv, local

    def copy(self, o):
        p, g = self.plan, self.g
        to = lax.rem(self.c + o, p.nc)
        cols = pl.ds(pl.multiple_of(to * p.width[g], 128), p.width[g])
        rows = pl.ds(pl.multiple_of(self.base + self.c * p.own, p.own), p.own)
        return remote(
            self.src.at[g, :, cols], self.dst.at[rows, :],
            self.send.at[g, o], self.recv.at[g, o], (self.r, to),
        )

    def arrive(self, o):
        p, g = self.plan, self.g
        frm = lax.rem(self.c + p.nc - o, p.nc)
        rows = pl.ds(pl.multiple_of(self.base + frm * p.own, p.own), p.own)
        return remote(
            self.src.at[g, :, pl.ds(0, p.width[g])], self.dst.at[rows, :],
            self.send.at[g, o], self.recv.at[g, o], (self.r, lax.rem(self.c + o, p.nc)),
        ), self.alive(frm)

    def alive(self, col):
        return self.r * self.plan.nc + col < self.plan.depth[self.g] // self.plan.own

    def mine(self):
        p, g = self.plan, self.g
        cols = pl.ds(pl.multiple_of(self.c * p.width[g], 128), p.width[g])
        rows = pl.ds(pl.multiple_of(self.base + self.c * p.own, p.own), p.own)
        return pltpu.make_async_copy(
            self.src.at[g, :, cols], self.dst.at[rows, :], self.local.at[g]
        )

    def start(self):
        @pl.when(self.alive(self.c))
        def _():
            for o in range(1, self.plan.nc):
                self.copy(o).start()
            self.mine().start()

    def wait_recv(self):
        for o in range(1, self.plan.nc):
            copy, ok = self.arrive(o)
            pl.when(ok)(copy.wait_recv)
        pl.when(self.alive(self.c))(self.mine().wait)

    def wait_send(self):
        @pl.when(self.alive(self.c))
        def _():
            for o in range(1, self.plan.nc):
                self.copy(o).wait_send()


class Gather:
    def __init__(self, plan, g, r, c, src, dst, send, recv, fsend, frecv, local):
        self.plan, self.g, self.r, self.c = plan, g, r, c
        self.src, self.dst = src, dst
        self.send, self.recv, self.fsend, self.frecv = send, recv, fsend, frecv
        self.local = local
        self.twin = c + 1 - 2 * lax.rem(c, 2)

    def alive(self, col):
        return self.r * self.plan.nc + col < self.plan.depth[self.g] // self.plan.own

    def mine(self):
        return self.src.at[self.g, :, pl.ds(0, self.plan.depth[self.g])]

    def rows(self, col):
        p = self.plan
        return self.dst.at[pl.ds(pl.multiple_of(col * p.own, p.own), p.own), :]

    def copy(self, o):
        to = lax.rem(self.c + o, self.plan.nc)
        return remote(
            self.mine(), self.rows(self.c), self.send.at[self.g, o // 2],
            self.recv.at[self.g, o // 2], (self.r, to),
        )

    def arrive(self, o):
        frm = lax.rem(self.c + self.plan.nc - o, self.plan.nc)
        return remote(
            self.mine(), self.rows(frm), self.send.at[self.g, o // 2],
            self.recv.at[self.g, o // 2], (self.r, lax.rem(self.c + o, self.plan.nc)),
        ), frm

    def forward(self, o):
        frm = lax.rem(self.c + self.plan.nc - o, self.plan.nc)
        src = self.mine() if o == 0 else self.rows(frm)
        return remote(
            src, self.rows(frm), self.fsend.at[self.g, o // 2],
            self.frecv.at[self.g, o // 2], (self.r, self.twin),
        ), frm

    def from_twin(self, o):
        frm = lax.rem(self.twin + self.plan.nc - o, self.plan.nc)
        return remote(
            self.mine(), self.rows(frm), self.fsend.at[self.g, o // 2],
            self.frecv.at[self.g, o // 2], (self.r, self.twin),
        ), frm

    def own_copy(self):
        return pltpu.make_async_copy(self.mine(), self.rows(self.c), self.local.at[self.g])

    def start(self):
        @pl.when(self.alive(self.c))
        def _():
            for o in range(2, self.plan.nc, 2):
                self.copy(o).start()
            self.forward(0)[0].start()
            self.own_copy().start()

    def relay(self):
        for o in range(2, self.plan.nc, 2):
            copy, frm = self.arrive(o)
            forward, _ = self.forward(o)

            @pl.when(self.alive(frm))
            def _(copy=copy, forward=forward):
                copy.wait_recv()
                forward.start()

    def finish(self):
        for o in range(0, self.plan.nc, 2):
            copy, frm = self.from_twin(o)
            pl.when(self.alive(frm))(copy.wait_recv)
        for o in range(0, self.plan.nc, 2):
            forward, frm = self.forward(o)
            pl.when(self.alive(frm))(forward.wait_send)

        @pl.when(self.alive(self.c))
        def _():
            for o in range(2, self.plan.nc, 2):
                self.copy(o).wait_send()
            self.own_copy().wait()


class Stack:
    def __init__(self, plan, g, r, c, src, src_base, dst, send, recv):
        self.plan, self.g, self.r, self.c = plan, g, r, c
        self.src, self.src_base, self.dst = src, src_base, dst
        self.send, self.recv = send, recv
        self.full = plan.depth[g] // plan.panel
        self.rest = plan.depth[g] % plan.panel

    def copy(self, o, frm, size):
        p, g = self.plan, self.g
        at = pl.multiple_of(frm * p.panel, p.panel)
        return remote(
            self.src.at[pl.ds(self.src_base, size), :], self.dst.at[pl.ds(at, size), :],
            self.send.at[g, o], self.recv.at[g, o], (lax.rem(self.r + o, p.nr), self.c),
        )

    def cases(self, frm, act):
        if self.full:
            pl.when(frm < self.full)(lambda: act(frm, self.plan.panel))
        if self.rest:
            pl.when(frm == self.full)(lambda: act(self.full, self.rest))

    def start(self):
        def act(frm, size):
            for o in range(1, self.plan.nr):
                self.copy(o, frm, size).start()
        self.cases(self.r, act)

    def wait_send(self):
        def act(frm, size):
            for o in range(1, self.plan.nr):
                self.copy(o, frm, size).wait_send()
        self.cases(self.r, act)

    def wait_recv(self):
        for o in range(1, self.plan.nr):
            frm = lax.rem(self.r + self.plan.nr - o, self.plan.nr)
            self.cases(frm, lambda f, size, o=o: self.recv_one(o, f, size))

    def recv_one(self, o, frm, size):
        p, g = self.plan, self.g
        at = pl.multiple_of(frm * p.panel, p.panel)
        remote(
            self.dst.at[pl.ds(at, size), :], self.dst.at[pl.ds(at, size), :],
            self.send.at[g, o], self.recv.at[g, o], (lax.rem(self.r + o, p.nr), self.c),
        ).wait_recv()


def first_kernel(plan, t, w, v, *refs):
    n = plan.blocks
    tcol, vpan, wgrid = refs[:n], refs[n : 2 * n], refs[2 * n : 3 * n]
    ts, tr, ws, wr, gs, gr, fs, fr, zs, zr, loc_t, loc_w, loc_v = refs[3 * n :]
    r, c = lax.axis_index("row"), lax.axis_index("col")
    barrier_line(plan, r, c)
    base = r * plan.panel
    at = pl.multiple_of(base, plan.panel)
    t_spread = [Spread(plan, g, r, c, t, tcol[g], base, ts, tr, loc_t) for g in range(n)]
    w_spread = [Spread(plan, g, r, c, w, wgrid[g], 0, ws, wr, loc_w) for g in range(n)]
    v_gather = [Gather(plan, g, r, c, v, vpan[g], gs, gr, fs, fr, loc_v) for g in range(n)]
    stack = [Stack(plan, g, r, c, tcol[g], at, tcol[g], zs, zr) for g in range(n)]
    for g in range(n):
        t_spread[g].start()
    for g in range(n):
        v_gather[g].start()
    for g in range(n):
        w_spread[g].start()
    for g in range(n):
        t_spread[g].wait_recv()
        stack[g].start()
    for g in range(n):
        v_gather[g].relay()
    for g in range(n):
        v_gather[g].finish()
        w_spread[g].wait_recv()
        w_spread[g].wait_send()
        t_spread[g].wait_send()
    for g in range(n):
        stack[g].wait_recv()
        stack[g].wait_send()


def second_kernel(plan, t, *refs):
    n = plan.blocks
    x, tpan, xcol = refs[:n], refs[n : 2 * n], refs[2 * n : 3 * n]
    gs, gr, fs, fr, zs, zr, loc_t, loc_x = refs[3 * n :]
    r, c = lax.axis_index("row"), lax.axis_index("col")
    barrier_line(plan, r, c)
    gather = [Gather(plan, g, r, c, t, tpan[g], gs, gr, fs, fr, loc_t) for g in range(n)]
    stack = [Stack(plan, g, r, c, x[g], 0, xcol[g], zs, zr) for g in range(n)]

    def place(g, act):
        def one(frm, size):
            at = pl.multiple_of(frm * plan.panel, plan.panel)
            act(pltpu.make_async_copy(
                x[g].at[pl.ds(0, size), :], xcol[g].at[pl.ds(at, size), :], loc_x.at[g]
            ))
        stack[g].cases(r, one)

    for g in range(n):
        stack[g].start()
    for g in range(n):
        gather[g].start()
        place(g, lambda copy: copy.start())
    for g in range(n):
        gather[g].relay()
    for g in range(n):
        gather[g].finish()
        place(g, lambda copy: copy.wait())
    for g in range(n):
        stack[g].wait_recv()
        stack[g].wait_send()


def third_kernel(plan, *refs):
    n = plan.blocks
    z, zt = refs[:n], refs[n : 2 * n]
    rows, mirror = refs[2 * n : 2 * n + 2]
    rs, rr, ms, mr, loc_r, loc_m = refs[2 * n + 2 :]
    r, c = lax.axis_index("row"), lax.axis_index("col")
    sem = pltpu.get_barrier_semaphore()
    total = plan.nr * plan.nc
    me = r * plan.nc + c

    @pl.loop(1, total)
    def _(o):
        to = lax.rem(me + o, total)
        pl.semaphore_signal(
            sem, inc=1, device_id=(to // plan.nc, lax.rem(to, plan.nc)), device_id_type=MESH
        )
    pl.semaphore_wait(sem, total - 1)

    own, panel = plan.own, plan.panel

    def row_copy(g, o):
        to = lax.rem(c + o, plan.nc)
        src = z[g].at[pl.ds(pl.multiple_of(to * own, own), own), :]
        dst = rows.at[g, :, pl.ds(pl.multiple_of(c * plan.width[g], 128), plan.width[g])]
        if o == 0:
            return pltpu.make_async_copy(src, dst, loc_r.at[g])
        return remote(src, dst, rs.at[g, o], rr.at[g, o], (r, to))

    def row_arrival(g, o):
        frm = lax.rem(c + plan.nc - o, plan.nc)
        dst = rows.at[g, :, pl.ds(pl.multiple_of(frm * plan.width[g], 128), plan.width[g])]
        return remote(dst, dst, rs.at[g, o], rr.at[g, o], (r, lax.rem(c + o, plan.nc)))

    def mirror_copy(g, p, act_here, act_there):
        parts = plan.width[g] // own
        to = c * parts + p
        src = zt[g].at[pl.ds(p * own, own), :]
        dst = mirror.at[g, :, pl.ds(pl.multiple_of(r * panel, panel), panel)]

        @pl.when(to == me)
        def _():
            act_here(pltpu.make_async_copy(src, dst, loc_m.at[g]))

        @pl.when((to != me) & (to < total))
        def _():
            act_there(remote(
                src, dst, ms.at[g, p], mr.at[g, r], (to // plan.nc, lax.rem(to, plan.nc))
            ))

    def nothing(copy):
        return None

    def mirror_arrival(g, q):
        parts = plan.width[g] // own
        frm = q * plan.nc + me // parts
        dst = mirror.at[g, :, pl.ds(q * panel, panel)]

        @pl.when((frm != me) & (me // parts < plan.nc))
        def _():
            remote(dst, dst, ms.at[g, 0], mr.at[g, q], (lax.rem(r + 1, plan.nr), c)).wait_recv()

    for g in range(n):
        for p in range(plan.width[g] // own):
            mirror_copy(g, p, lambda copy: copy.start(), lambda copy: copy.start())
    for g in range(n):
        for o in range(plan.nc):
            row_copy(g, o).start()
    for g in range(n):
        for o in range(plan.nc):
            if o == 0:
                row_copy(g, o).wait()
            else:
                row_arrival(g, o).wait_recv()
                row_copy(g, o).wait_send()
        for q in range(plan.nr):
            mirror_arrival(g, q)
        for p in range(plan.width[g] // own):
            mirror_copy(g, p, lambda copy: copy.wait(), lambda copy: copy.wait_send())


def call(kernel, plan, outs, sems, number, *args):
    any_space = pl.BlockSpec(memory_space=pl.ANY)
    return pl.pallas_call(
        functools.partial(kernel, plan),
        out_shape=outs,
        in_specs=[any_space] * len(args),
        out_specs=[any_space] * len(outs),
        scratch_shapes=[pltpu.SemaphoreType.DMA(s) for s in sems],
        compiler_params=pltpu.CompilerParams(collective_id=number, has_side_effects=True),
    )(*args)


def body(mesh, t_amps, w_cycle, v_cycle, occ_irrep, vir_irrep, e_occ, e_vir):
    counts = block_counts(occ_irrep.shape[0], vir_irrep.shape[0], t_amps.shape[0])
    plan = Plan(mesh, t_amps.shape, counts)
    n, own, panel, nr, nc = plan.blocks, plan.own, plan.panel, plan.nr, plan.nc
    r = lax.axis_index("row")
    device = lax.axis_index(("row", "col"))
    limit = jnp.array(counts, jnp.int32)
    slot = jnp.arange(plan.slots, dtype=jnp.int32)
    my_slot = device * own + jnp.arange(own, dtype=jnp.int32)
    row_alive = my_slot[None, :] < limit[:, None]
    alive = slot[None, :] < limit[:, None]
    pair_energy = pair_table(occ_irrep, vir_irrep, e_occ, e_vir, counts, plan.slots)

    def half(*shape):
        return jax.ShapeDtypeStruct(shape, jnp.bfloat16)

    t_rows = jnp.where(row_alive[:, :, None], t_amps, jnp.zeros((), jnp.bfloat16))
    groups = range(n)
    column = [half(plan.depth[g], plan.width[g]) for g in groups]
    tile = [half(panel, plan.width[g]) for g in groups]
    rowpan = [half(panel, plan.depth[g]) for g in groups]
    plane, pair, line, one = (n, nc), (n, nc // 2), (n, nr), (n,)
    got = call(
        first_kernel, plan, column + rowpan + tile,
        [plane] * 4 + [pair] * 4 + [line] * 2 + [one] * 3, 1, t_rows, w_cycle, v_cycle,
    )
    tcol, vpan, wgrid = got[:n], got[n : 2 * n], got[2 * n :]
    panel_slot = r * panel + jnp.arange(panel, dtype=jnp.int32)
    x = []
    for g in groups:
        product = jnp.dot(vpan[g], tcol[g], preferred_element_type=jnp.float32)
        x_tile = (wgrid[g].astype(jnp.float32) + 0.5 * product).astype(jnp.bfloat16)
        x.append(jnp.where((panel_slot < counts[g])[:, None], x_tile, jnp.zeros((), jnp.bfloat16)))
    got = call(
        second_kernel, plan, rowpan + column, [pair] * 4 + [line] * 2 + [one] * 2, 2, t_rows, *x
    )
    tpan, xcol = got[:n], got[n:]
    z, zt = [], []
    for g in groups:
        z_tile = jnp.dot(tpan[g], xcol[g], preferred_element_type=jnp.float32).astype(jnp.bfloat16)
        z.append(z_tile)
        zt.append(z_tile.T)
    parts = max(plan.width) // own
    z_rows, z_mirror = call(
        third_kernel, plan, [half(n, own, plan.slots)] * 2,
        [plane] * 2 + [(n, parts), line] + [one] * 2, 3, *z, *zt,
    )
    row_energy = lax.dynamic_slice_in_dim(pair_energy, device * own, own, 1)
    denom = row_energy[:, :, None] + pair_energy[:, None, :]
    numer = v_cycle.astype(jnp.float32) + z_rows.astype(jnp.float32) + z_mirror.astype(jnp.float32)
    live = row_alive[:, :, None] & alive[:, None, :]
    return jnp.where(live, numer / denom, jnp.zeros((), jnp.float32))


def solution(mesh):
    rows = P(None, ("row", "col"), None)
    return jax.shard_map(
        functools.partial(body, mesh), mesh=mesh,
        in_specs=(rows, rows, rows, P(), P(), P(), P()), out_specs=rows, check_vma=False,
    )
```

```python
import functools

import jax
import jax.numpy as jnp
from jax import lax
from jax.experimental import pallas as pl
from jax.experimental.pallas import tpu as pltpu
from jax.sharding import PartitionSpec as P

OCC_CUM = (12, 16, 24, 29, 33, 39, 45, 50)
VIR_CUM = (100, 145, 220, 275, 315, 380, 445, 500)
MESH = pl.DeviceIdType.MESH


def block_counts(n_occ, n_vir, blocks):
    occ = [n_occ * c // 50 for c in OCC_CUM]
    vir = [n_vir * c // 500 for c in VIR_CUM]
    occ = [b - a for a, b in zip([0] + occ, occ)]
    vir = [b - a for a, b in zip([0] + vir, vir)]
    return [sum(occ[h] * vir[h ^ g] for h in range(8)) for g in range(blocks)]


def pair_table(occ_irrep, vir_irrep, e_occ, e_vir, counts, slots):
    blocks = len(counts)
    n_occ = occ_irrep.shape[0]
    group = jnp.arange(blocks, dtype=jnp.int32)
    want = jnp.bitwise_xor(vir_irrep[None, :], group[:, None])
    per = jnp.sum((want[:, :, None] == occ_irrep[None, None, :]).astype(jnp.int32), axis=2)
    n_vir = vir_irrep.shape[0]
    before = jnp.arange(n_vir)[:, None] < jnp.arange(n_vir)[None, :]
    first = jnp.sum(jnp.where(before[None], per[:, :, None], 0), axis=1)
    slot = jnp.arange(slots, dtype=jnp.int32)[None, None, :]
    offset = slot - first[:, :, None]
    hit = (offset >= 0) & (offset < per[:, :, None])
    place = jnp.sum(jnp.where(hit, offset * 8 + want[:, :, None], 0), axis=1)
    e_a = jnp.sum(jnp.where(hit, e_vir[None, :, None], 0.0), axis=1)
    earlier = jnp.arange(n_occ)[:, None] < jnp.arange(n_occ)[None, :]
    rank = jnp.sum((earlier & (occ_irrep[:, None] == occ_irrep[None, :])).astype(jnp.int32), axis=0)
    key = rank * 8 + occ_irrep
    e_i = jnp.sum(
        jnp.where(place[:, None, :] == key[None, :, None], e_occ[None, :, None], 0.0), axis=1
    )
    filled = slot[0] < jnp.array(counts, jnp.int32)[:, None]
    return jnp.where(filled, e_i - e_a, -1.0)


class Plan:
    def __init__(self, mesh, shape, counts):
        self.nr, self.nc = mesh.shape["row"], mesh.shape["col"]
        self.blocks, self.slots = shape[0], shape[2]
        self.own = self.slots // (self.nr * self.nc)
        self.panel = self.own * self.nc
        self.counts = counts
        self.depth = [-(-n // 128) * 128 for n in counts]
        self.width = [-(-k // (128 * self.nc)) * 128 for k in self.depth]

    def planes(self, g):
        return -(-self.depth[g] // self.panel)

    def rows(self, g, s):
        return min(self.panel, self.depth[g] - s * self.panel)


def barrier_line(plan, r, c):
    sem = pltpu.get_barrier_semaphore()
    for o in range(1, plan.nc):
        pl.semaphore_signal(
            sem, inc=1, device_id=(r, lax.rem(c + o, plan.nc)), device_id_type=MESH
        )
    for o in range(1, plan.nr):
        pl.semaphore_signal(
            sem, inc=1, device_id=(lax.rem(r + o, plan.nr), c), device_id_type=MESH
        )
    pl.semaphore_wait(sem, plan.nc + plan.nr - 2)


def remote(src, dst, send, recv, device):
    return pltpu.make_async_remote_copy(
        src_ref=src, dst_ref=dst, send_sem=send, recv_sem=recv, device_id=device, device_id_type=MESH
    )


class Spread:
    def __init__(self, plan, g, r, c, src, dst, base, send, recv, local):
        self.plan, self.g, self.r, self.c = plan, g, r, c
        self.src, self.dst, self.base = src, dst, base
        self.send, self.recv, self.local = send, recv, local

    def rows(self, col):
        p = self.plan
        return pl.ds(pl.multiple_of(self.base + col * p.own, p.own), p.own)

    def pieces(self, to):
        p, g = self.plan, self.g
        for b in range(p.width[g] // 128):
            cols = pl.ds(pl.multiple_of((b * p.nc + to) * 128, 128), 128)
            yield self.src.at[g, :, cols], self.dst.at[self.rows(self.c), pl.ds(b * 128, 128)]

    def whole(self, o, col):
        ref = self.dst.at[self.rows(col), :]
        to = lax.rem(self.c + o, self.plan.nc)
        return remote(ref, ref, self.send.at[self.g, o], self.recv.at[self.g, o], (self.r, to))

    def alive(self, col):
        return self.r * self.plan.nc + col < self.plan.depth[self.g] // self.plan.own

    def start(self):
        @pl.when(self.alive(self.c))
        def _():
            for o in range(1, self.plan.nc):
                to = lax.rem(self.c + o, self.plan.nc)
                for src, dst in self.pieces(to):
                    remote(
                        src, dst, self.send.at[self.g, o], self.recv.at[self.g, o], (self.r, to)
                    ).start()
            for src, dst in self.pieces(self.c):
                pltpu.make_async_copy(src, dst, self.local.at[self.g]).start()

    def wait_recv(self):
        for o in range(1, self.plan.nc):
            frm = lax.rem(self.c + self.plan.nc - o, self.plan.nc)
            pl.when(self.alive(frm))(self.whole(o, frm).wait_recv)

        @pl.when(self.alive(self.c))
        def _():
            ref = self.dst.at[self.rows(self.c), :]
            pltpu.make_async_copy(ref, ref, self.local.at[self.g]).wait()

    def wait_send(self):
        @pl.when(self.alive(self.c))
        def _():
            for o in range(1, self.plan.nc):
                self.whole(o, self.c).wait_send()


class Gather:
    def __init__(self, plan, g, r, c, src, dst, send, recv, fsend, frecv, local):
        self.plan, self.g, self.r, self.c = plan, g, r, c
        self.src, self.dst = src, dst
        self.send, self.recv, self.fsend, self.frecv = send, recv, fsend, frecv
        self.local = local
        self.twin = c + 1 - 2 * lax.rem(c, 2)

    def alive(self, col):
        return self.r * self.plan.nc + col < self.plan.depth[self.g] // self.plan.own

    def mine(self):
        return self.src.at[self.g, :, pl.ds(0, self.plan.depth[self.g])]

    def rows(self, col):
        p = self.plan
        return self.dst.at[pl.ds(pl.multiple_of(col * p.own, p.own), p.own), :]

    def copy(self, o):
        to = lax.rem(self.c + o, self.plan.nc)
        return remote(
            self.mine(), self.rows(self.c), self.send.at[self.g, o // 2],
            self.recv.at[self.g, o // 2], (self.r, to),
        )

    def arrive(self, o):
        frm = lax.rem(self.c + self.plan.nc - o, self.plan.nc)
        return remote(
            self.mine(), self.rows(frm), self.send.at[self.g, o // 2],
            self.recv.at[self.g, o // 2], (self.r, lax.rem(self.c + o, self.plan.nc)),
        ), frm

    def forward(self, o):
        frm = lax.rem(self.c + self.plan.nc - o, self.plan.nc)
        src = self.mine() if o == 0 else self.rows(frm)
        return remote(
            src, self.rows(frm), self.fsend.at[self.g, o // 2],
            self.frecv.at[self.g, o // 2], (self.r, self.twin),
        ), frm

    def from_twin(self, o):
        frm = lax.rem(self.twin + self.plan.nc - o, self.plan.nc)
        return remote(
            self.mine(), self.rows(frm), self.fsend.at[self.g, o // 2],
            self.frecv.at[self.g, o // 2], (self.r, self.twin),
        ), frm

    def own_copy(self):
        return pltpu.make_async_copy(self.mine(), self.rows(self.c), self.local.at[self.g])

    def start(self):
        @pl.when(self.alive(self.c))
        def _():
            for o in range(2, self.plan.nc, 2):
                self.copy(o).start()
            self.forward(0)[0].start()
            self.own_copy().start()

    def relay(self):
        for o in range(2, self.plan.nc, 2):
            copy, frm = self.arrive(o)
            forward, _ = self.forward(o)

            @pl.when(self.alive(frm))
            def _(copy=copy, forward=forward):
                copy.wait_recv()
                forward.start()

    def finish(self):
        for o in range(0, self.plan.nc, 2):
            copy, frm = self.from_twin(o)
            pl.when(self.alive(frm))(copy.wait_recv)
        for o in range(0, self.plan.nc, 2):
            forward, frm = self.forward(o)
            pl.when(self.alive(frm))(forward.wait_send)

        @pl.when(self.alive(self.c))
        def _():
            for o in range(2, self.plan.nc, 2):
                self.copy(o).wait_send()
            self.own_copy().wait()


class Stack:
    def __init__(self, plan, g, r, c, src, dst, send, recv):
        self.plan, self.g, self.r, self.c = plan, g, r, c
        self.src, self.dst, self.send, self.recv = src, dst, send, recv
        self.planes = plan.planes(g)

    def rows(self, s):
        return self.dst.at[pl.ds(s * self.plan.panel, self.plan.rows(self.g, s)), :]

    def copy(self, s, up, first):
        size = self.plan.rows(self.g, s)
        src = self.src.at[pl.ds(0, size), :] if first and self.src is not None else self.rows(s)
        to = lax.rem(self.r + (1 if up else self.plan.nr - 1), self.plan.nr)
        return remote(
            src, self.rows(s), self.send.at[self.g, s, int(up)], self.recv.at[self.g, s],
            (to, self.c),
        )

    def pass_on(self, r, s, act):
        if r >= s and r + 1 < self.planes:
            act(self.copy(s, True, r == s))
        if r <= s and r > 0:
            act(self.copy(s, False, r == s))

    def start(self):
        for s in range(self.planes):
            pl.when(self.r == s)(lambda s=s: self.pass_on(s, s, lambda copy: copy.start()))

    def step(self, far):
        for r in range(self.planes):
            @pl.when(self.r == r)
            def _(r=r):
                for s in (r - far, r + far):
                    if 0 <= s < self.planes:
                        self.copy(s, s > r, False).wait_recv()
                        self.pass_on(r, s, lambda copy: copy.start())

    def wait_send(self):
        for r in range(self.planes):
            @pl.when(self.r == r)
            def _(r=r):
                for s in range(self.planes):
                    self.pass_on(r, s, lambda copy: copy.wait_send())


def first_kernel(plan, t, w, v, *refs):
    n = plan.blocks
    tcol, vpan, wgrid = refs[:n], refs[n : 2 * n], refs[2 * n : 3 * n]
    ts, tr, ws, wr, gs, gr, fs, fr, zs, zr, loc_t, loc_w, loc_v = refs[3 * n :]
    r, c = lax.axis_index("row"), lax.axis_index("col")
    barrier_line(plan, r, c)
    base = r * plan.panel
    t_spread = [Spread(plan, g, r, c, t, tcol[g], base, ts, tr, loc_t) for g in range(n)]
    w_spread = [Spread(plan, g, r, c, w, wgrid[g], 0, ws, wr, loc_w) for g in range(n)]
    v_gather = [Gather(plan, g, r, c, v, vpan[g], gs, gr, fs, fr, loc_v) for g in range(n)]
    stack = [Stack(plan, g, r, c, None, tcol[g], zs, zr) for g in range(n)]
    for g in range(n):
        t_spread[g].start()
    for g in range(n):
        t_spread[g].wait_recv()
        stack[g].start()
        v_gather[g].start()
    for g in range(n):
        w_spread[g].start()
    for far in range(1, plan.nr):
        for g in range(n):
            stack[g].step(far)
            if far == min(2, plan.nr - 1):
                v_gather[g].relay()
    for g in range(n):
        v_gather[g].finish()
        w_spread[g].wait_recv()
        w_spread[g].wait_send()
        t_spread[g].wait_send()
        stack[g].wait_send()


def second_kernel(plan, t, *refs):
    n = plan.blocks
    x, tpan, xcol = refs[:n], refs[n : 2 * n], refs[2 * n : 3 * n]
    gs, gr, fs, fr, zs, zr, loc_t, loc_x = refs[3 * n :]
    r, c = lax.axis_index("row"), lax.axis_index("col")
    barrier_line(plan, r, c)
    gather = [Gather(plan, g, r, c, t, tpan[g], gs, gr, fs, fr, loc_t) for g in range(n)]
    stack = [Stack(plan, g, r, c, x[g], xcol[g], zs, zr) for g in range(n)]

    def place(g, act):
        for s in range(plan.planes(g)):
            @pl.when(r == s)
            def _(s=s):
                size = plan.rows(g, s)
                act(pltpu.make_async_copy(
                    x[g].at[pl.ds(0, size), :], stack[g].rows(s), loc_x.at[g]
                ))

    for g in range(n):
        stack[g].start()
    for g in range(n):
        gather[g].start()
        place(g, lambda copy: copy.start())
    for far in range(1, plan.nr):
        for g in range(n):
            stack[g].step(far)
            if far == min(2, plan.nr - 1):
                gather[g].relay()
    for g in range(n):
        gather[g].finish()
        place(g, lambda copy: copy.wait())
        stack[g].wait_send()


def third_kernel(plan, *refs):
    n = plan.blocks
    z, zt = refs[:n], refs[n : 2 * n]
    rows, mirror = refs[2 * n : 2 * n + 2]
    rs, rr, ms, mr, loc_r, loc_m = refs[2 * n + 2 :]
    r, c = lax.axis_index("row"), lax.axis_index("col")
    own, panel, nr, nc = plan.own, plan.panel, plan.nr, plan.nc
    total, sub = nr * nc, 128 // own
    me = r * nc + c
    if sub == 1:
        barrier_line(plan, r, c)
    else:
        sem = pltpu.get_barrier_semaphore()

        @pl.loop(1, total)
        def _(o):
            to = lax.rem(me + o, total)
            pl.semaphore_signal(
                sem, inc=1, device_id=(to // nc, lax.rem(to, nc)), device_id_type=MESH
            )
        pl.semaphore_wait(sem, total - 1)

    def row_pieces(g, to):
        for b in range(plan.width[g] // 128):
            src = z[g].at[pl.ds(pl.multiple_of(to * own, own), own), pl.ds(b * 128, 128)]
            yield src, rows.at[g, :, pl.ds(pl.multiple_of((b * nc + c) * 128, 128), 128)]

    def row_alive(g, col):
        return r * nc + col < plan.depth[g] // own

    def row_whole(g, o):
        ref = rows.at[g, :, pl.ds(0, plan.width[g])]
        return remote(ref, ref, rs.at[g, o], rr.at[g, o], (r, lax.rem(c + o, nc)))

    def start_rows(g):
        for o in range(nc):
            to = lax.rem(c + o, nc)

            @pl.when(row_alive(g, to))
            def _(o=o, to=to):
                for src, dst in row_pieces(g, to):
                    if o:
                        remote(src, dst, rs.at[g, o], rr.at[g, o], (r, to)).start()
                    else:
                        pltpu.make_async_copy(src, dst, loc_r.at[g]).start()

    def end_rows(g):
        @pl.when(row_alive(g, c))
        def _():
            for o in range(1, nc):
                row_whole(g, o).wait_recv()
            ref = rows.at[g, :, pl.ds(0, plan.width[g])]
            pltpu.make_async_copy(ref, ref, loc_r.at[g]).wait()
        for o in range(1, nc):
            pl.when(row_alive(g, lax.rem(c + o, nc)))(row_whole(g, o).wait_send)

    def mirror_copies(g, here, there):
        for s in range(plan.planes(g)):
            @pl.when(r == s)
            def _(s=s):
                size = plan.rows(g, s)
                for p in range(plan.width[g] // own):
                    to = ((p // sub) * nc + c) * sub + p % sub
                    src = zt[g].at[pl.ds(p * own, own), pl.ds(0, size)]
                    dst = mirror.at[g, :, pl.ds(s * panel, size)]
                    far = remote(
                        src, dst, ms.at[g, p], mr.at[g, s], (to // nc, lax.rem(to, nc))
                    )
                    near = pltpu.make_async_copy(src, dst, loc_m.at[g])
                    fits = to < plan.depth[g] // own
                    pl.when((to == me) & fits)(functools.partial(here, near))
                    pl.when((to != me) & fits)(functools.partial(there, far))

    def mirror_arrivals(g):
        for s in range(plan.planes(g)):
            frm = s * nc + lax.rem(me // sub, nc)
            dst = mirror.at[g, :, pl.ds(s * panel, plan.rows(g, s))]
            copy = remote(dst, dst, ms.at[g, 0], mr.at[g, s], (lax.rem(r + 1, nr), c))
            pl.when((frm != me) & (me < plan.depth[g] // own))(copy.wait_recv)

    for g in range(n):
        mirror_copies(g, lambda copy: copy.start(), lambda copy: copy.start())
    for g in range(n):
        start_rows(g)
    for g in range(n):
        end_rows(g)
        mirror_arrivals(g)
        mirror_copies(g, lambda copy: copy.wait(), lambda copy: copy.wait_send())


def call(kernel, plan, outs, sems, number, *args):
    any_space = pl.BlockSpec(memory_space=pl.ANY)
    return pl.pallas_call(
        functools.partial(kernel, plan),
        out_shape=outs,
        in_specs=[any_space] * len(args),
        out_specs=[any_space] * len(outs),
        scratch_shapes=[pltpu.SemaphoreType.DMA(s) for s in sems],
        compiler_params=pltpu.CompilerParams(collective_id=number, has_side_effects=True),
    )(*args)


def body(mesh, t_amps, w_cycle, v_cycle, occ_irrep, vir_irrep, e_occ, e_vir):
    counts = block_counts(occ_irrep.shape[0], vir_irrep.shape[0], t_amps.shape[0])
    plan = Plan(mesh, t_amps.shape, counts)
    n, own, panel, nr, nc = plan.blocks, plan.own, plan.panel, plan.nr, plan.nc
    r = lax.axis_index("row")
    device = lax.axis_index(("row", "col"))
    limit = jnp.array(counts, jnp.int32)
    slot = jnp.arange(plan.slots, dtype=jnp.int32)
    my_slot = device * own + jnp.arange(own, dtype=jnp.int32)
    row_alive = my_slot[None, :] < limit[:, None]
    alive = slot[None, :] < limit[:, None]
    pair_energy = pair_table(occ_irrep, vir_irrep, e_occ, e_vir, counts, plan.slots)

    def half(*shape):
        return jax.ShapeDtypeStruct(shape, jnp.bfloat16)

    t_rows = jnp.where(row_alive[:, :, None], t_amps, jnp.zeros((), jnp.bfloat16))
    groups = range(n)
    column = [half(plan.depth[g], plan.width[g]) for g in groups]
    tile = [half(panel, plan.width[g]) for g in groups]
    rowpan = [half(panel, plan.depth[g]) for g in groups]
    plane, pair, line, one = (n, nc), (n, nc // 2), (n, nr), (n,)
    both = (n, nr, 2)
    got = call(
        first_kernel, plan, column + rowpan + tile,
        [plane] * 4 + [pair] * 4 + [both, line] + [one] * 3, 1, t_rows, w_cycle, v_cycle,
    )
    tcol, vpan, wgrid = got[:n], got[n : 2 * n], got[2 * n :]
    panel_slot = r * panel + jnp.arange(panel, dtype=jnp.int32)
    x = []
    for g in groups:
        product = jnp.dot(vpan[g], tcol[g], preferred_element_type=jnp.float32)
        x_tile = (wgrid[g].astype(jnp.float32) + 0.5 * product).astype(jnp.bfloat16)
        x.append(jnp.where((panel_slot < counts[g])[:, None], x_tile, jnp.zeros((), jnp.bfloat16)))
    got = call(
        second_kernel, plan, rowpan + column, [pair] * 4 + [both, line] + [one] * 2, 2, t_rows, *x
    )
    tpan, xcol = got[:n], got[n:]
    z, zt = [], []
    for g in groups:
        z_tile = jnp.dot(tpan[g], xcol[g], preferred_element_type=jnp.float32).astype(jnp.bfloat16)
        z.append(z_tile)
        zt.append(z_tile.T)
    parts = max(plan.width) // own
    z_rows, z_mirror = call(
        third_kernel, plan, [half(n, own, plan.slots)] * 2,
        [plane] * 2 + [(n, parts), line] + [one] * 2, 3, *z, *zt,
    )
    row_energy = lax.dynamic_slice_in_dim(pair_energy, device * own, own, 1)
    denom = row_energy[:, :, None] + pair_energy[:, None, :]
    numer = v_cycle.astype(jnp.float32) + z_rows.astype(jnp.float32) + z_mirror.astype(jnp.float32)
    live = row_alive[:, :, None] & alive[:, None, :]
    return jnp.where(live, numer / denom, jnp.zeros((), jnp.float32))


def solution(mesh):
    rows = P(None, ("row", "col"), None)
    return jax.shard_map(
        functools.partial(body, mesh), mesh=mesh,
        in_specs=(rows, rows, rows, P(), P(), P(), P()), out_specs=rows, check_vma=False,
    )
```

```python
import functools

import jax
import jax.numpy as jnp
from jax import lax
from jax.experimental import pallas as pl
from jax.experimental.pallas import tpu as pltpu
from jax.sharding import PartitionSpec as P

OCC_CUM = (12, 16, 24, 29, 33, 39, 45, 50)
VIR_CUM = (100, 145, 220, 275, 315, 380, 445, 500)
MESH = pl.DeviceIdType.MESH


def block_counts(n_occ, n_vir, blocks):
    occ = [n_occ * c // 50 for c in OCC_CUM]
    vir = [n_vir * c // 500 for c in VIR_CUM]
    occ = [b - a for a, b in zip([0] + occ, occ)]
    vir = [b - a for a, b in zip([0] + vir, vir)]
    return [sum(occ[h] * vir[h ^ g] for h in range(8)) for g in range(blocks)]


def pair_table(occ_irrep, vir_irrep, e_occ, e_vir, counts, slots):
    blocks = len(counts)
    n_occ = occ_irrep.shape[0]
    group = jnp.arange(blocks, dtype=jnp.int32)
    want = jnp.bitwise_xor(vir_irrep[None, :], group[:, None])
    per = jnp.sum((want[:, :, None] == occ_irrep[None, None, :]).astype(jnp.int32), axis=2)
    n_vir = vir_irrep.shape[0]
    before = jnp.arange(n_vir)[:, None] < jnp.arange(n_vir)[None, :]
    first = jnp.sum(jnp.where(before[None], per[:, :, None], 0), axis=1)
    slot = slots[None, None, :]
    offset = slot - first[:, :, None]
    hit = (offset >= 0) & (offset < per[:, :, None])
    place = jnp.sum(jnp.where(hit, offset * 8 + want[:, :, None], 0), axis=1)
    e_a = jnp.sum(jnp.where(hit, e_vir[None, :, None], 0.0), axis=1)
    earlier = jnp.arange(n_occ)[:, None] < jnp.arange(n_occ)[None, :]
    rank = jnp.sum((earlier & (occ_irrep[:, None] == occ_irrep[None, :])).astype(jnp.int32), axis=0)
    key = rank * 8 + occ_irrep
    e_i = jnp.sum(
        jnp.where(place[:, None, :] == key[None, :, None], e_occ[None, :, None], 0.0), axis=1
    )
    filled = slot[0] < jnp.array(counts, jnp.int32)[:, None]
    return jnp.where(filled, e_i - e_a, -1.0)


class Plan:
    def __init__(self, mesh, shape, counts):
        self.nr, self.nc = mesh.shape["row"], mesh.shape["col"]
        self.blocks, self.slots = shape[0], shape[2]
        self.own = self.slots // (self.nr * self.nc)
        self.panel = self.own * self.nc
        self.counts = counts
        self.depth = [-(-n // 128) * 128 for n in counts]
        self.width = [-(-k // (128 * self.nc)) * 128 for k in self.depth]

    def place(self, g, col):
        return lax.rem(col + self.nc // 2, self.nc) if g % 3 == 2 else col

    def planes(self, g):
        return -(-self.depth[g] // self.panel)

    def rows(self, g, s):
        return min(self.panel, self.depth[g] - s * self.panel)


def barrier_line(plan, r, c, across=0):
    sem = pltpu.get_barrier_semaphore()
    for o in range(1, plan.nc):
        pl.semaphore_signal(
            sem, inc=1, device_id=(r, lax.rem(c + o, plan.nc)), device_id_type=MESH
        )
    for o in range(1, plan.nr):
        pl.semaphore_signal(
            sem, inc=1, device_id=(lax.rem(r + o, plan.nr), c), device_id_type=MESH
        )
        if across:
            pl.semaphore_signal(
                sem, inc=1, device_id=(lax.rem(r + o, plan.nr), lax.rem(c + across, plan.nc)),
                device_id_type=MESH,
            )
    pl.semaphore_wait(sem, plan.nc - 1 + (plan.nr - 1) * (2 if across else 1))


def remote(src, dst, send, recv, device):
    return pltpu.make_async_remote_copy(
        src_ref=src, dst_ref=dst, send_sem=send, recv_sem=recv, device_id=device, device_id_type=MESH
    )


class Spread:
    def __init__(self, plan, g, r, c, src, dst, base, send, recv, local):
        self.plan, self.g, self.r, self.c = plan, g, r, c
        self.src, self.dst, self.base = src, dst, base
        self.send, self.recv, self.local = send, recv, local

    def rows(self, col):
        p = self.plan
        return pl.ds(pl.multiple_of(self.base + col * p.own, p.own), p.own)

    def pieces(self, to):
        p, g = self.plan, self.g
        for b in range(p.width[g] // 128):
            cols = pl.ds(pl.multiple_of((b * p.nc + p.place(g, to)) * 128, 128), 128)
            yield self.src.at[g, :, cols], self.dst.at[self.rows(self.c), pl.ds(b * 128, 128)]

    def whole(self, o, col):
        ref = self.dst.at[self.rows(col), :]
        to = lax.rem(self.c + o, self.plan.nc)
        return remote(ref, ref, self.send.at[self.g, o], self.recv.at[self.g, o], (self.r, to))

    def alive(self, col):
        return self.r * self.plan.nc + col < self.plan.depth[self.g] // self.plan.own

    def start(self):
        @pl.when(self.alive(self.c))
        def _():
            for o in range(1, self.plan.nc):
                to = lax.rem(self.c + o, self.plan.nc)
                for src, dst in self.pieces(to):
                    remote(
                        src, dst, self.send.at[self.g, o], self.recv.at[self.g, o], (self.r, to)
                    ).start()
            for src, dst in self.pieces(self.c):
                pltpu.make_async_copy(src, dst, self.local.at[self.g]).start()

    def wait_recv(self):
        for o in range(1, self.plan.nc):
            frm = lax.rem(self.c + self.plan.nc - o, self.plan.nc)
            pl.when(self.alive(frm))(self.whole(o, frm).wait_recv)

        @pl.when(self.alive(self.c))
        def _():
            ref = self.dst.at[self.rows(self.c), :]
            pltpu.make_async_copy(ref, ref, self.local.at[self.g]).wait()

    def wait_send(self):
        @pl.when(self.alive(self.c))
        def _():
            for o in range(1, self.plan.nc):
                self.whole(o, self.c).wait_send()


class Gather:
    def __init__(self, plan, g, r, c, src, dst, send, recv, fsend, frecv, local):
        self.plan, self.g, self.r, self.c = plan, g, r, c
        self.src, self.dst = src, dst
        self.send, self.recv, self.fsend, self.frecv = send, recv, fsend, frecv
        self.local = local
        self.twin = c + 1 - 2 * lax.rem(c, 2)

    def alive(self, col):
        return self.r * self.plan.nc + col < self.plan.depth[self.g] // self.plan.own

    def mine(self):
        return self.src.at[self.g, :, pl.ds(0, self.plan.depth[self.g])]

    def rows(self, col):
        p = self.plan
        return self.dst.at[pl.ds(pl.multiple_of(col * p.own, p.own), p.own), :]

    def copy(self, o):
        to = lax.rem(self.c + o, self.plan.nc)
        return remote(
            self.mine(), self.rows(self.c), self.send.at[self.g, o // 2],
            self.recv.at[self.g, o // 2], (self.r, to),
        )

    def arrive(self, o):
        frm = lax.rem(self.c + self.plan.nc - o, self.plan.nc)
        return remote(
            self.mine(), self.rows(frm), self.send.at[self.g, o // 2],
            self.recv.at[self.g, o // 2], (self.r, lax.rem(self.c + o, self.plan.nc)),
        ), frm

    def forward(self, o):
        frm = lax.rem(self.c + self.plan.nc - o, self.plan.nc)
        src = self.mine() if o == 0 else self.rows(frm)
        return remote(
            src, self.rows(frm), self.fsend.at[self.g, o // 2],
            self.frecv.at[self.g, o // 2], (self.r, self.twin),
        ), frm

    def from_twin(self, o):
        frm = lax.rem(self.twin + self.plan.nc - o, self.plan.nc)
        return remote(
            self.mine(), self.rows(frm), self.fsend.at[self.g, o // 2],
            self.frecv.at[self.g, o // 2], (self.r, self.twin),
        ), frm

    def own_copy(self):
        return pltpu.make_async_copy(self.mine(), self.rows(self.c), self.local.at[self.g])

    def start(self):
        @pl.when(self.alive(self.c))
        def _():
            for o in range(2, self.plan.nc, 2):
                self.copy(o).start()
            self.forward(0)[0].start()
            self.own_copy().start()

    def relay(self):
        for o in range(2, self.plan.nc, 2):
            copy, frm = self.arrive(o)
            forward, _ = self.forward(o)

            @pl.when(self.alive(frm))
            def _(copy=copy, forward=forward):
                copy.wait_recv()
                forward.start()

    def finish(self):
        for o in range(0, self.plan.nc, 2):
            copy, frm = self.from_twin(o)
            pl.when(self.alive(frm))(copy.wait_recv)
        for o in range(0, self.plan.nc, 2):
            forward, frm = self.forward(o)
            pl.when(self.alive(frm))(forward.wait_send)

        @pl.when(self.alive(self.c))
        def _():
            for o in range(2, self.plan.nc, 2):
                self.copy(o).wait_send()
            self.own_copy().wait()


class Stack:
    def __init__(self, plan, g, r, c, src, dst, send, recv):
        self.plan, self.g, self.r, self.c = plan, g, r, c
        self.src, self.dst, self.send, self.recv = src, dst, send, recv
        self.planes = plan.planes(g)

    def rows(self, s):
        at = pl.ds(s * self.plan.panel, self.plan.rows(self.g, s))
        return self.dst.at[at, pl.ds(0, self.live)]

    def each_width(self, act):
        p, width = self.plan, self.plan.width[self.g]
        rest = p.depth[self.g] // 128 % p.nc
        at = p.place(self.g, self.c)

        def run(live):
            self.live = live
            act()

        if rest:
            pl.when(at < rest)(lambda: run(width))
            if width > 128:
                pl.when(at >= rest)(lambda: run(width - 128))
        else:
            run(width)

    def copy(self, s, up, first):
        size = self.plan.rows(self.g, s)
        src = self.rows(s)
        if first and self.src is not None:
            src = self.src.at[pl.ds(0, size), pl.ds(0, self.live)]
        to = lax.rem(self.r + (1 if up else self.plan.nr - 1), self.plan.nr)
        return remote(
            src, self.rows(s), self.send.at[self.g, s, int(up)], self.recv.at[self.g, s],
            (to, self.c),
        )

    def pass_on(self, r, s, act):
        if r >= s and r + 1 < self.planes:
            act(self.copy(s, True, r == s))
        if r <= s and r > 0:
            act(self.copy(s, False, r == s))

    def start(self):
        self.each_width(self.start_one)

    def step(self, far):
        self.each_width(lambda: self.step_one(far))

    def wait_send(self):
        self.each_width(self.wait_send_one)

    def start_one(self):
        for s in range(self.planes):
            pl.when(self.r == s)(lambda s=s: self.pass_on(s, s, lambda copy: copy.start()))

    def step_one(self, far):
        for r in range(self.planes):
            @pl.when(self.r == r)
            def _(r=r):
                for s in (r - far, r + far):
                    if 0 <= s < self.planes:
                        self.copy(s, s > r, False).wait_recv()
                        self.pass_on(r, s, lambda copy: copy.start())

    def wait_send_one(self):
        for r in range(self.planes):
            @pl.when(self.r == r)
            def _(r=r):
                for s in range(self.planes):
                    self.pass_on(r, s, lambda copy: copy.wait_send())


def first_kernel(plan, t, w, v, *refs):
    n = plan.blocks
    tcol, vpan, wgrid = refs[:n], refs[n : 2 * n], refs[2 * n : 3 * n]
    ts, tr, ws, wr, gs, gr, fs, fr, zs, zr, loc_t, loc_w, loc_v = refs[3 * n :]
    r, c = lax.axis_index("row"), lax.axis_index("col")
    barrier_line(plan, r, c)
    base = r * plan.panel
    t_spread = [Spread(plan, g, r, c, t, tcol[g], base, ts, tr, loc_t) for g in range(n)]
    w_spread = [Spread(plan, g, r, c, w, wgrid[g], 0, ws, wr, loc_w) for g in range(n)]
    v_gather = [Gather(plan, g, r, c, v, vpan[g], gs, gr, fs, fr, loc_v) for g in range(n)]
    stack = [Stack(plan, g, r, c, None, tcol[g], zs, zr) for g in range(n)]
    for g in range(n):
        t_spread[g].start()
    for g in range(n):
        t_spread[g].wait_recv()
        stack[g].start()
        v_gather[g].start()
    for g in range(n):
        w_spread[g].start()
    for far in range(1, plan.nr):
        for g in range(n):
            stack[g].step(far)
            if far == min(2, plan.nr - 1):
                v_gather[g].relay()
    for g in range(n):
        v_gather[g].finish()
        w_spread[g].wait_recv()
        w_spread[g].wait_send()
        t_spread[g].wait_send()
        stack[g].wait_send()


def second_kernel(plan, t, *refs):
    n = plan.blocks
    x, tpan, xcol = refs[:n], refs[n : 2 * n], refs[2 * n : 3 * n]
    gs, gr, fs, fr, zs, zr, loc_t, loc_x = refs[3 * n :]
    r, c = lax.axis_index("row"), lax.axis_index("col")
    barrier_line(plan, r, c)
    gather = [Gather(plan, g, r, c, t, tpan[g], gs, gr, fs, fr, loc_t) for g in range(n)]
    stack = [Stack(plan, g, r, c, x[g], xcol[g], zs, zr) for g in range(n)]

    def place(g, act):
        for s in range(plan.planes(g)):
            @pl.when(r == s)
            def _(s=s):
                size = plan.rows(g, s)
                act(pltpu.make_async_copy(
                    x[g].at[pl.ds(0, size), :], xcol[g].at[pl.ds(s * plan.panel, size), :],
                    loc_x.at[g]
                ))

    for g in range(n):
        stack[g].start()
    for g in range(n):
        gather[g].start()
        place(g, lambda copy: copy.start())
    for far in range(1, plan.nr):
        for g in range(n):
            stack[g].step(far)
            if far == min(2, plan.nr - 1):
                gather[g].relay()
    for g in range(n):
        gather[g].finish()
        place(g, lambda copy: copy.wait())
        stack[g].wait_send()


def third_kernel(plan, *refs):
    n = plan.blocks
    z, zt = refs[:n], refs[n : 2 * n]
    rows, mirror = refs[2 * n : 2 * n + 2]
    rs, rr, ms, mr, loc_r, loc_m = refs[2 * n + 2 :]
    r, c = lax.axis_index("row"), lax.axis_index("col")
    own, panel, nr, nc = plan.own, plan.panel, plan.nr, plan.nc
    total, sub = nr * nc, 128 // own
    me = r * nc + c
    if sub == 1:
        barrier_line(plan, r, c, nc // 2)
    else:
        sem = pltpu.get_barrier_semaphore()

        @pl.loop(1, total)
        def _(o):
            to = lax.rem(me + o, total)
            pl.semaphore_signal(
                sem, inc=1, device_id=(to // nc, lax.rem(to, nc)), device_id_type=MESH
            )
        pl.semaphore_wait(sem, total - 1)

    def row_pieces(g, to):
        for b in range(plan.width[g] // 128):
            src = z[g].at[pl.ds(pl.multiple_of(to * own, own), own), pl.ds(b * 128, 128)]
            yield src, rows.at[g, :, pl.ds(pl.multiple_of((b * nc + plan.place(g, c)) * 128, 128), 128)]

    def row_alive(g, col):
        return r * nc + col < plan.depth[g] // own

    def row_whole(g, o):
        ref = rows.at[g, :, pl.ds(0, plan.width[g])]
        return remote(ref, ref, rs.at[g, o], rr.at[g, o], (r, lax.rem(c + o, nc)))

    def start_rows(g):
        for o in range(nc):
            to = lax.rem(c + o, nc)

            @pl.when(row_alive(g, to))
            def _(o=o, to=to):
                for src, dst in row_pieces(g, to):
                    if o:
                        remote(src, dst, rs.at[g, o], rr.at[g, o], (r, to)).start()
                    else:
                        pltpu.make_async_copy(src, dst, loc_r.at[g]).start()

    def end_rows(g):
        @pl.when(row_alive(g, c))
        def _():
            for o in range(1, nc):
                row_whole(g, o).wait_recv()
            ref = rows.at[g, :, pl.ds(0, plan.width[g])]
            pltpu.make_async_copy(ref, ref, loc_r.at[g]).wait()
        for o in range(1, nc):
            pl.when(row_alive(g, lax.rem(c + o, nc)))(row_whole(g, o).wait_send)

    def mirror_copies(g, here, there):
        for s in range(plan.planes(g)):
            @pl.when(r == s)
            def _(s=s):
                size = plan.rows(g, s)
                for p in range(plan.width[g] // own):
                    to = ((p // sub) * nc + plan.place(g, c)) * sub + p % sub
                    src = zt[g].at[pl.ds(p * own, own), pl.ds(0, size)]
                    dst = mirror.at[g, :, pl.ds(s * panel, size)]
                    far = remote(
                        src, dst, ms.at[g, p], mr.at[g, s], (to // nc, lax.rem(to, nc))
                    )
                    near = pltpu.make_async_copy(src, dst, loc_m.at[g])
                    fits = to < plan.depth[g] // own
                    pl.when((to == me) & fits)(functools.partial(here, near))
                    pl.when((to != me) & fits)(functools.partial(there, far))

    def mirror_arrivals(g):
        for s in range(plan.planes(g)):
            frm = s * nc + plan.place(g, lax.rem(me // sub, nc))
            dst = mirror.at[g, :, pl.ds(s * panel, plan.rows(g, s))]
            copy = remote(dst, dst, ms.at[g, 0], mr.at[g, s], (lax.rem(r + 1, nr), c))
            pl.when((frm != me) & (me < plan.depth[g] // own))(copy.wait_recv)

    for g in range(n):
        mirror_copies(g, lambda copy: copy.start(), lambda copy: copy.start())
    for g in range(n):
        start_rows(g)
    for g in range(n):
        end_rows(g)
        mirror_arrivals(g)
        mirror_copies(g, lambda copy: copy.wait(), lambda copy: copy.wait_send())


def call(kernel, plan, outs, sems, number, *args):
    any_space = pl.BlockSpec(memory_space=pl.ANY)
    return pl.pallas_call(
        functools.partial(kernel, plan),
        out_shape=outs,
        in_specs=[any_space] * len(args),
        out_specs=[any_space] * len(outs),
        scratch_shapes=[pltpu.SemaphoreType.DMA(s) for s in sems],
        compiler_params=pltpu.CompilerParams(collective_id=number, has_side_effects=True),
    )(*args)


def body(mesh, t_amps, w_cycle, v_cycle, occ_irrep, vir_irrep, e_occ, e_vir):
    counts = block_counts(occ_irrep.shape[0], vir_irrep.shape[0], t_amps.shape[0])
    plan = Plan(mesh, t_amps.shape, counts)
    n, own, panel, nr, nc = plan.blocks, plan.own, plan.panel, plan.nr, plan.nc
    r = lax.axis_index("row")
    device = lax.axis_index(("row", "col"))
    limit = jnp.array(counts, jnp.int32)
    slot = jnp.arange(plan.slots, dtype=jnp.int32)
    my_slot = device * own + jnp.arange(own, dtype=jnp.int32)
    row_alive = my_slot[None, :] < limit[:, None]
    alive = slot[None, :] < limit[:, None]
    row_energy = pair_table(occ_irrep, vir_irrep, e_occ, e_vir, counts, my_slot)
    pair_energy = lax.all_gather(row_energy, ("row", "col"), axis=1, tiled=True)

    def half(*shape):
        return jax.ShapeDtypeStruct(shape, jnp.bfloat16)

    t_rows = jnp.where(row_alive[:, :, None], t_amps, jnp.zeros((), jnp.bfloat16))
    groups = range(n)
    column = [half(plan.depth[g], plan.width[g]) for g in groups]
    tile = [half(panel, plan.width[g]) for g in groups]
    rowpan = [half(panel, plan.depth[g]) for g in groups]
    plane, pair, line, one = (n, nc), (n, nc // 2), (n, nr), (n,)
    both = (n, nr, 2)
    got = call(
        first_kernel, plan, column + rowpan + tile,
        [plane] * 4 + [pair] * 4 + [both, line] + [one] * 3, 1, t_rows, w_cycle, v_cycle,
    )
    tcol, vpan, wgrid = got[:n], got[n : 2 * n], got[2 * n :]
    panel_slot = r * panel + jnp.arange(panel, dtype=jnp.int32)
    x = []
    for g in groups:
        product = jnp.dot(vpan[g], tcol[g], preferred_element_type=jnp.float32)
        x_tile = (wgrid[g].astype(jnp.float32) + 0.5 * product).astype(jnp.bfloat16)
        x.append(jnp.where((panel_slot < counts[g])[:, None], x_tile, jnp.zeros((), jnp.bfloat16)))
    got = call(
        second_kernel, plan, rowpan + column, [pair] * 4 + [both, line] + [one] * 2, 2, t_rows, *x
    )
    tpan, xcol = got[:n], got[n:]
    z, zt = [], []
    for g in groups:
        z_tile = jnp.dot(tpan[g], xcol[g], preferred_element_type=jnp.float32).astype(jnp.bfloat16)
        z.append(z_tile)
        zt.append(z_tile.T)
    parts = max(plan.width) // own
    z_rows, z_mirror = call(
        third_kernel, plan, [half(n, own, plan.slots)] * 2,
        [plane] * 2 + [(n, parts), line] + [one] * 2, 3, *z, *zt,
    )
    denom = row_energy[:, :, None] + pair_energy[:, None, :]
    numer = v_cycle.astype(jnp.float32) + z_rows.astype(jnp.float32) + z_mirror.astype(jnp.float32)
    live = row_alive[:, :, None] & alive[:, None, :]
    return jnp.where(live, numer / denom, jnp.zeros((), jnp.float32))


def solution(mesh):
    rows = P(None, ("row", "col"), None)
    return jax.shard_map(
        functools.partial(body, mesh), mesh=mesh,
        in_specs=(rows, rows, rows, P(), P(), P(), P()), out_specs=rows, check_vma=False,
    )
```
